32 devices in a mesh: clip: 8 (over y, x, core), row: 4 (over z).
Axes of the slice: x: 2, y: 2, z: 4, core: 2. Of those that a mesh axis runs over, the one named last changes fastest.
Arguments:
- video_clips: bfloat16 [8, 4, 16, 64, 512], P('clip', None, 'row'), may hold values from -60 to 60
- norm_gain: float32 [512], replicated, may hold values from 0.1 to 1.9
- norm_bias: float32 [512], replicated, may hold values from -3 to 3
- spatial_weight: bfloat16 [4608, 512], P('clip'), may hold values from -0.09375 to 0.09375
- spatial_bias: float32 [512], replicated, may hold values from -3 to 3
- temporal_weight: bfloat16 [1536, 512], P('clip'), may hold values from -0.15625 to 0.15625
- temporal_bias: float32 [512], replicated, may hold values from -3 to 3
Outputs:
- encoded: bfloat16 [8, 2, 16, 64, 512], P('clip', None, 'row')
The draws below stay inside these ranges and needn't reach their ends.
All inputs are finite; a program needn't handle non-finite values.
Results may differ from the reference program's by a relative error of at most 0.0025.
Values may be sent and summed in bfloat16 or wider, within the bound.
A program may use at most 64 MiB of HBM per device.

```python
import math
import jax
import jax.numpy as jnp
from jax import lax

C = 512
GROUPS = 32
FRAMES = 4
COLS = 64
CLIPS = 8
HEIGHT = 16


def draw_video_clips(key, part):
    keys = jax.random.split(jax.random.fold_in(key, 11), 3)
    shape = (CLIPS, FRAMES, HEIGHT, COLS, C)
    channel_scale = jnp.exp(jax.random.uniform(keys[1], (C,), jnp.float32, math.log(0.3), math.log(3.0)))
    height_pos = jnp.arange(HEIGHT, dtype=jnp.float32) / max(HEIGHT - 1, 1)
    jitter = jnp.exp(jax.random.uniform(keys[2], (CLIPS, FRAMES, HEIGHT, 1, 1), jnp.float32, math.log(0.7), math.log(1.4)))
    row_scale = jnp.exp(math.log(3.0) * height_pos)
    base = jax.random.truncated_normal(keys[0], -4.0, 4.0, shape, jnp.float32) + 0.5
    values = base * channel_scale * row_scale[None, None, :, None, None] * jitter
    return values.astype(jnp.bfloat16)


def level_of(own_key, extent, shards, low, largest):
    loudness, own = 1.0, jax.random.fold_in(own_key, 6)
    for position, blocks in shards:
        steps = jnp.exp(jax.random.uniform(jax.random.fold_in(own, position), (blocks,), jnp.float32, low / len(shards), largest / len(shards)))
        loudness = loudness * jnp.repeat(steps, extent[position] // blocks).reshape([-1 if axis == position else 1 for axis in range(len(extent))])
    return loudness


def bell_draw(key, extent, deviation, most, cuts=(), kind=jnp.bfloat16):
    drawn = deviation * jax.random.normal(key, extent, jnp.float32)
    if cuts:
        drawn = drawn * level_of(key, extent, cuts, -0.22, 0.18)
    return jnp.clip(drawn, -most, most).astype(kind)


def setup_inputs(seed: int = 0) -> dict:
    key_of = jax.random.split(jax.random.key(seed), 8)
    video_clips = draw_video_clips(jax.random.fold_in(key_of[7], 71), 0)
    norm_gain = jnp.clip(1.0 + 0.18 * jax.random.normal(key_of[1], (C,), jnp.float32), 0.1, 1.9)
    norm_bias = bell_draw(key_of[2], (C,), 0.5, 3.0, (), jnp.float32)
    spatial_weight = bell_draw(key_of[3], (9 * C, C), (9 * C) ** -0.5, 0.09375, ((0, 8),))
    spatial_bias = bell_draw(key_of[4], (C,), 0.5, 3.0, (), jnp.float32)
    temporal_weight = bell_draw(key_of[5], (3 * C, C), (3 * C) ** -0.5, 0.15625, ((0, 8),))
    temporal_bias = bell_draw(key_of[6], (C,), 0.5, 3.0, (), jnp.float32)
    return {"video_clips": video_clips, "norm_gain": norm_gain, "norm_bias": norm_bias, "spatial_weight": spatial_weight, "spatial_bias": spatial_bias, "temporal_weight": temporal_weight, "temporal_bias": temporal_bias}


def reference(video_clips, norm_gain, norm_bias, spatial_weight, spatial_bias, temporal_weight, temporal_bias):
    group_width = C // GROUPS
    population = FRAMES * HEIGHT * COLS * group_width

    def one_clip(single):
        widened = single.astype(jnp.float32)
        grouped = widened.reshape(FRAMES * HEIGHT * COLS, GROUPS, group_width)
        group_mean = lax.optimization_barrier(jnp.sum(grouped, axis=(0, 2))) / population
        squares = lax.optimization_barrier(jnp.sum(grouped * grouped, axis=(0, 2))) / population
        group_spread = squares - group_mean * group_mean
        inverse = lax.rsqrt(group_spread + 1e-06)
        mean_chan = jnp.repeat(group_mean, group_width)
        inverse_chan = jnp.repeat(inverse, group_width)
        normed = (widened - mean_chan) * inverse_chan * norm_gain + norm_bias
        activated = jax.nn.silu(normed).astype(jnp.bfloat16)
        padded = jnp.pad(activated, ((0, 0), (1, 1), (1, 1), (0, 0)))
        accum = jnp.zeros((FRAMES * HEIGHT * COLS, C), jnp.float32)
        for row_shift in range(3):
            for col_shift in range(3):
                tap_index = 3 * row_shift + col_shift
                window = padded[:, row_shift:row_shift + HEIGHT, col_shift:col_shift + COLS].reshape(-1, C)
                accum = accum + jnp.dot(window, spatial_weight[tap_index * C:(tap_index + 1) * C], preferred_element_type=jnp.float32)
        middle = (accum + spatial_bias).astype(jnp.bfloat16).reshape(FRAMES, HEIGHT, COLS, C)
        time_padded = jnp.concatenate([middle[:1], middle[:1], middle], axis=0)
        result = jnp.zeros((FRAMES // 2 * HEIGHT * COLS, C), jnp.float32)
        for tap_index in range(3):
            window = time_padded[tap_index:tap_index + FRAMES:2].reshape(-1, C)
            result = result + jnp.dot(window, temporal_weight[tap_index * C:(tap_index + 1) * C], preferred_element_type=jnp.float32)
        input_padded = jnp.concatenate([widened[:1], widened], axis=0)
        pooled = 0.5 * (input_padded[0:FRAMES:2] + input_padded[1:FRAMES + 1:2])
        result = result.reshape(FRAMES // 2, HEIGHT, COLS, C) + temporal_bias + pooled
        return result.astype(jnp.bfloat16)
    return lax.map(one_clip, video_clips)
```

```python
import functools

import jax
import jax.numpy as jnp
from jax import lax
from jax.experimental import pallas as pl
from jax.experimental.pallas import tpu as pltpu
from jax.sharding import PartitionSpec as P

GROUPS = 32
MESH = pl.DeviceIdType.MESH


def group_total(values, group_width):
    lanes = values.shape[1]
    step = 1
    while step < group_width:
        values = values + pltpu.roll(values, step, 1)
        step *= 2
    lane = lax.broadcasted_iota(jnp.int32, values.shape, 1)
    values = jnp.where(lane % group_width == group_width - 1, values, 0.0)
    step = 1
    while step < group_width:
        values = values + pltpu.roll(values, lanes - step, 1)
        step *= 2
    return values


def z_rows(rows):
    return max(rows // 64 * 16, 16)


def kernel(
    n_clip, n_row,
    x, gain, bias, spatial, spatial_bias, temporal, temporal_bias,
    out,
    spatial_full, temporal_full, act, acc, halo, stats,
    send_sems, recv_sems, local_sems,
):
    me, row = lax.axis_index("clip"), lax.axis_index("row")
    parity = row % 2
    _, frames, height, cols, channels = x.shape
    used = acc.shape[0]
    group_width = channels // GROUPS
    half = channels // 2
    bits = n_clip.bit_length() - 1
    chip_bits = [1 << k for k in range(1, bits)]
    orders = (chip_bits, chip_bits[::-1])
    own = (spatial, temporal)
    full = (spatial_full, temporal_full)

    def flip(index, mask):
        for k in range(bits):
            if mask >> k & 1:
                index = index + (1 - 2 * (index // (1 << k) % 2)) * (1 << k)
        return index

    sibling, layer = (flip(me, 1), row), (me, flip(row, 1))

    barrier = pltpu.get_barrier_semaphore()
    greeted = [(flip(me, 1 << k), row) for k in range(bits)]
    greeted += [(me, lax.rem(row + d, n_row)) for d in range(1, n_row)]
    for device in greeted:
        pl.semaphore_signal(barrier, inc=1, device_id=device, device_id_type=MESH)
    pl.semaphore_wait(barrier, len(greeted))

    arrivals, departures = {}, []

    def send(key, source, target, landing, device):
        slot = len(departures)
        copy = pltpu.make_async_remote_copy(
            src_ref=source, dst_ref=target, send_sem=send_sems.at[slot],
            recv_sem=recv_sems.at[slot], device_id=device, device_id_type=MESH,
        )
        copy.start()
        departures.append(copy)
        arrivals[key] = pltpu.make_async_remote_copy(
            src_ref=landing, dst_ref=landing, send_sem=send_sems.at[slot],
            recv_sem=recv_sems.at[slot], device_id=device, device_id_type=MESH,
        )

    def span(which, kind):
        rows = own[which].shape[0]
        edge = z_rows(rows)
        if kind == "mine":
            return parity * (rows - edge), edge
        if kind == "theirs":
            return (1 - parity) * (rows - edge), edge
        if kind == "direct":
            return edge, rows - 2 * edge
        return 0, rows

    def part(which, shard, kind, order=None):
        start, size = span(which, kind)
        base = pl.multiple_of(shard * own[which].shape[0] + start, 16)
        columns = slice(None) if order is None else pl.ds(order * half, half)
        return full[which].at[pl.ds(base, size), columns]

    def own_part(which, kind, order=None):
        start, size = span(which, kind)
        columns = slice(None) if order is None else pl.ds(order * half, half)
        if not isinstance(start, int):
            start = pl.multiple_of(start, 16)
        return own[which].at[pl.ds(start, size), columns]

    def hop(which, kind, order, stage, mask):
        bit = orders[order][stage]
        shard = flip(me, mask)
        source = own_part(which, kind, order) if mask == 0 else part(which, shard, kind, order)
        send(
            (which, kind, order, stage, mask), source, part(which, shard, kind, order),
            part(which, flip(shard, bit), kind, order), (flip(me, bit), row),
        )

    def send_own(which, kind):
        for stage in range(bits - 1):
            for order in range(2):
                hop(which, kind, order, stage, 0)

    def share(which, kind, mask):
        shard = flip(me, mask)
        source = part(which, shard, kind) if mask else own[which]
        send(
            (which, kind, "s", mask), source, part(which, shard, kind),
            part(which, flip(shard, 1), kind), sibling,
        )

    even_masks = range(2, n_clip, 2)

    def pump(which, kind, depth):
        for order in range(2):
            line = orders[order]
            for stage in range(bits - 1):
                earlier = sum(line[:stage])
                for mask in range(0, n_clip, 2):
                    gained = mask | line[stage]
                    if mask & ~earlier or gained.bit_count() != depth:
                        continue
                    arrivals[which, kind, order, stage, mask].wait_recv()
                    for later in range(stage + 1, bits - 1):
                        hop(which, kind, order, later, gained)
        for mask in even_masks:
            if mask.bit_count() == depth:
                if kind == "mine":
                    shard = flip(me, mask)
                    send(
                        (which, "z", mask), part(which, shard, "mine"),
                        part(which, shard, "mine"), part(which, shard, "theirs"), layer,
                    )
                share(which, kind, mask)

    def settle(which, depth):
        for mask in even_masks:
            if mask.bit_count() == depth:
                arrivals[which, "z", mask].wait_recv()
                share(which, "theirs", mask)

    def from_sibling(which, masks):
        for mask in masks:
            for kind in ("mine", "direct", "theirs") if mask else ("all",):
                arrivals[which, kind, "s", mask].wait_recv()

    def edge_copy(slot, source_row, target, device):
        return pltpu.make_async_remote_copy(
            src_ref=x.at[0, pl.ds(0, used), source_row], dst_ref=halo.at[target],
            send_sem=local_sems.at[2 + slot], recv_sem=local_sems.at[4 + slot],
            device_id=device, device_id_type=MESH,
        )

    down = edge_copy(0, height - 1, 0, (me, lax.rem(row + 1, n_row)))
    up = edge_copy(1, 0, 1, (me, lax.rem(row + n_row - 1, n_row)))
    has_above, has_below = row > 0, row < n_row - 1

    send_own(0, "mine")
    pl.when(has_below)(down.start)
    pl.when(has_above)(up.start)
    send_own(0, "direct")
    share(0, "all", 0)
    locals_ = [
        pltpu.make_async_copy(own[w], part(w, me, "all"), local_sems.at[w]) for w in range(2)
    ]
    for copy in locals_:
        copy.start()

    tiles = frames * height
    population = tiles * cols * group_width

    def tile(index):
        return x[0, index // height, index % height].astype(jnp.float32)

    def fold(values):
        return jnp.sum(values.reshape(cols // 8, 8, channels), axis=0)

    zeros = jnp.zeros((8, channels), jnp.float32)
    total = lax.fori_loop(0, tiles, lambda k, s: s + fold(tile(k)), zeros, unroll=2)
    total = jnp.broadcast_to(jnp.sum(total, axis=0, keepdims=True), (8, channels))
    near_mean = group_total(total, group_width) / population

    def squares(k, s):
        centred = tile(k) - near_mean[:1]
        return s + fold(centred * centred)

    square = lax.fori_loop(0, tiles, squares, zeros, unroll=2)
    square = jnp.broadcast_to(jnp.sum(square, axis=0, keepdims=True), (8, channels))
    near_square = group_total(square, group_width)
    line = lax.broadcasted_iota(jnp.int32, (8, channels), 0)
    stats[0] = jnp.where(line < 4, near_mean, near_square)
    for d in range(1, n_row):
        send(("stats", d), stats.at[0], stats.at[d], stats.at[d], (me, lax.rem(row + d, n_row)))

    pump(0, "mine", 1)
    send_own(1, "mine")

    for d in range(1, n_row):
        arrivals["stats", d].wait_recv()
    means = [stats[d, 0:1] for d in range(n_row)]
    mean = sum(means) / n_row
    spread = sum(stats[d, 4:5] for d in range(n_row))
    spread = spread + population * sum((m - mean) * (m - mean) for m in means)
    inverse = lax.rsqrt(spread / (population * n_row) + 1e-06)

    place = lax.broadcasted_iota(jnp.int32, (cols, channels), 0)

    def put(frame, line, values):
        for b, moved in enumerate((
            jnp.where(place == 0, 0.0, pltpu.roll(values, 1, 0)),
            values,
            jnp.where(place == cols - 1, 0.0, pltpu.roll(values, cols - 1, 0)),
        )):
            moved = moved.astype(jnp.bfloat16)
            for c in range(2):
                act[b, c, frame, line] = moved[:, c * half:(c + 1) * half]

    def activate(values):
        normed = (values - mean) * inverse * gain[...] + bias[...]
        return normed / (1.0 + jnp.exp(-normed))

    @pl.loop(0, used * height)
    def _(index):
        frame, line = index // height, index % height
        put(frame, line + 1, activate(x[0, frame, line].astype(jnp.float32)))

    pump(0, "direct", 1)
    send_own(1, "direct")
    share(1, "all", 0)
    for depth in range(2, bits):
        pump(0, "mine", depth)

    for present, copy, target in ((has_above, down, 0), (has_below, up, 1)):
        line = target * (height + 1)

        @pl.when(present)
        def _():
            copy.wait_recv()

            @pl.loop(0, used)
            def _(frame):
                put(frame, line, activate(halo[target, frame].astype(jnp.float32)))

        @pl.when(jnp.logical_not(present))
        def _():
            @pl.loop(0, used)
            def _(frame):
                for b in range(3):
                    for c in range(2):
                        act[b, c, frame, line] = jnp.zeros((cols, half), jnp.bfloat16)

    quarter = me // (n_clip // 4)

    def convolve(phase, blocks):
        @pl.loop(0, used)
        def _(frame):
            value = None
            for block in blocks:
                tap, c = block // 2, block % 2
                window = act[tap % 3, c, frame, pl.ds(tap // 3, height)]
                rows = pl.ds(pl.multiple_of(block * half, half), half)
                product = jnp.dot(
                    window.reshape(height * cols, half), spatial_full[rows, :],
                    preferred_element_type=jnp.float32,
                )
                value = product if value is None else value + product
            acc[frame] = value + (spatial_bias[...] if phase == 0 else acc[frame])

    def blocks_of(phase):
        spot = quarter
        if phase & 1:
            spot = spot + 1 - 2 * (spot % 2)
        if phase & 2:
            spot = (spot + 2) % 4
        first = (9 * spot + 1) // 2
        chosen = [first + k for k in range(4)]
        if phase & 1:
            chosen.append(spot // 2 * 9 + 4)
        return chosen

    def of_phase(phase):
        return [m for m in range(0, n_clip, 2) if m >> (bits - 2) == phase]

    locals_[0].wait()
    early = n_clip == 8
    if early:
        from_sibling(0, of_phase(0))
        convolve(0, blocks_of(0))
    pump(1, "mine", 1)
    for depth in range(2, bits):
        pump(0, "direct", depth)
    for depth in range(1, bits):
        settle(0, depth)
    pump(1, "direct", 1)
    for depth in range(2, bits):
        pump(1, "mine", depth)
    if not early:
        from_sibling(0, of_phase(0))
        convolve(0, blocks_of(0))
    for phase in (1, 2):
        from_sibling(0, of_phase(phase))
        convolve(phase, blocks_of(phase))
    for depth in range(2, bits):
        pump(1, "direct", depth)
    for depth in range(1, bits):
        settle(1, depth)
    from_sibling(0, of_phase(3))
    convolve(3, blocks_of(3))

    locals_[1].wait()
    from_sibling(1, range(0, n_clip, 2))

    def tap_product(k, frame):
        return jnp.dot(
            acc[frame].astype(jnp.bfloat16), temporal_full[k * channels:(k + 1) * channels, :],
            preferred_element_type=jnp.float32,
        )

    for j in range(frames // 2):
        before, at = max(2 * j - 1, 0), 2 * j
        pooled = 0.5 * (x[0, before].astype(jnp.float32) + x[0, at].astype(jnp.float32))
        value = sum(tap_product(k, max(2 * j + k - 2, 0)) for k in range(3))
        value = value + temporal_bias[...] + pooled.reshape(height * cols, channels)
        out[0, j] = value.reshape(height, cols, channels).astype(out.dtype)

    for copy in departures:
        copy.wait_send()
    pl.when(has_below)(down.wait_send)
    pl.when(has_above)(up.wait_send)


def body(
    n_clip, n_row,
    video_clips, norm_gain, norm_bias, spatial_weight, spatial_bias, temporal_weight, temporal_bias,
):
    _, frames, height, cols, channels = video_clips.shape
    used = frames - 1
    half = channels // 2
    shards = n_clip // 2 - 1
    copies = 2 * (4 * shards + shards + 3 * shards + 1) + n_row - 1
    vmem = pl.BlockSpec(memory_space=pltpu.VMEM)
    hbm = pl.BlockSpec(memory_space=pl.ANY)
    flat = lambda v: v.reshape(1, channels)
    return pl.pallas_call(
        functools.partial(kernel, n_clip, n_row),
        out_shape=jax.ShapeDtypeStruct((1, frames // 2, height, cols, channels), jnp.bfloat16),
        in_specs=[vmem, vmem, vmem, hbm, vmem, hbm, vmem],
        out_specs=vmem,
        scratch_shapes=[
            pltpu.VMEM((9 * channels, channels), jnp.bfloat16),
            pltpu.VMEM((3 * channels, channels), jnp.bfloat16),
            pltpu.VMEM((3, 2, used, height + 2, cols, half), jnp.bfloat16),
            pltpu.VMEM((used, height * cols, channels), jnp.float32),
            pltpu.VMEM((2, used, cols, channels), jnp.bfloat16),
            pltpu.VMEM((n_row, 8, channels), jnp.float32),
            pltpu.SemaphoreType.DMA((copies,)),
            pltpu.SemaphoreType.DMA((copies,)),
            pltpu.SemaphoreType.DMA((6,)),
        ],
        compiler_params=pltpu.CompilerParams(
            collective_id=0, has_side_effects=True, vmem_limit_bytes=40 * 1024 * 1024
        ),
    )(
        video_clips, flat(norm_gain), flat(norm_bias), spatial_weight, flat(spatial_bias),
        temporal_weight, flat(temporal_bias),
    )


def solution(mesh):
    placed = (
        P("clip", None, "row", None, None),
        P(),
        P(),
        P("clip", None),
        P(),
        P("clip", None),
        P(),
    )
    return jax.shard_map(
        functools.partial(body, mesh.shape["clip"], mesh.shape["row"]),
        mesh=mesh,
        in_specs=placed,
        out_specs=P("clip", None, "row", None, None),
        check_vma=False,
    )
```

```python
import functools

import jax
import jax.numpy as jnp
from jax import lax
from jax.experimental import pallas as pl
from jax.experimental.pallas import tpu as pltpu
from jax.sharding import PartitionSpec as P

GROUPS = 32
MESH = pl.DeviceIdType.MESH


def group_total(values, group_width):
    lanes = values.shape[1]
    step = 1
    while step < group_width:
        values = values + pltpu.roll(values, step, 1)
        step *= 2
    lane = lax.broadcasted_iota(jnp.int32, values.shape, 1)
    values = jnp.where(lane % group_width == group_width - 1, values, 0.0)
    step = 1
    while step < group_width:
        values = values + pltpu.roll(values, lanes - step, 1)
        step *= 2
    return values


def z_rows(rows):
    return max(rows // 64 * 16, 16)


def kernel(
    n_clip, n_row,
    clips, gain_in, bias_in, spatial, spatial_bias_in, temporal, temporal_bias_in,
    out,
    x, gain, bias, spatial_bias, temporal_bias,
    spatial_full, temporal_full, act, acc, halo, stats,
    send_sems, recv_sems, local_sems,
):
    me, row = lax.axis_index("clip"), lax.axis_index("row")
    parity = row % 2
    _, frames, height, cols, channels = clips.shape
    used = acc.shape[0]
    group_width = channels // GROUPS
    half = channels // 2
    bits = n_clip.bit_length() - 1
    chip_bits = [1 << k for k in range(1, bits)]
    orders = (chip_bits, chip_bits[::-1])
    own = (spatial, temporal)
    full = (spatial_full, temporal_full)

    def flip(index, mask):
        for k in range(bits):
            if mask >> k & 1:
                index = index + (1 - 2 * (index // (1 << k) % 2)) * (1 << k)
        return index

    sibling, layer = (flip(me, 1), row), (me, flip(row, 1))

    fetch = pltpu.make_async_copy(clips, x, local_sems.at[6])
    fetch.start()
    vectors = [
        pltpu.make_async_copy(source, target, local_sems.at[7 + k])
        for k, (source, target) in enumerate((
            (gain_in, gain), (bias_in, bias),
            (spatial_bias_in, spatial_bias), (temporal_bias_in, temporal_bias),
        ))
    ]
    for copy in vectors:
        copy.start()

    barrier = pltpu.get_barrier_semaphore()
    greeted = [(flip(me, 1 << k), row) for k in range(bits)]
    greeted += [(me, lax.rem(row + d, n_row)) for d in range(1, n_row)]
    for device in greeted:
        pl.semaphore_signal(barrier, inc=1, device_id=device, device_id_type=MESH)
    pl.semaphore_wait(barrier, len(greeted))

    arrivals, departures = {}, []

    def send(key, source, target, landing, device):
        slot = len(departures)
        copy = pltpu.make_async_remote_copy(
            src_ref=source, dst_ref=target, send_sem=send_sems.at[slot],
            recv_sem=recv_sems.at[slot], device_id=device, device_id_type=MESH,
        )
        copy.start()
        departures.append(copy)
        arrivals[key] = pltpu.make_async_remote_copy(
            src_ref=landing, dst_ref=landing, send_sem=send_sems.at[slot],
            recv_sem=recv_sems.at[slot], device_id=device, device_id_type=MESH,
        )

    def span(which, kind):
        rows = own[which].shape[0]
        edge = z_rows(rows)
        if kind == "mine":
            return parity * (rows - edge), edge
        if kind == "theirs":
            return (1 - parity) * (rows - edge), edge
        if kind == "direct":
            return edge, rows - 2 * edge
        return 0, rows

    def part(which, shard, kind, order=None):
        start, size = span(which, kind)
        base = pl.multiple_of(shard * own[which].shape[0] + start, 16)
        columns = slice(None) if order is None else pl.ds(order * half, half)
        return full[which].at[pl.ds(base, size), columns]

    def own_part(which, kind, order=None):
        start, size = span(which, kind)
        columns = slice(None) if order is None else pl.ds(order * half, half)
        if not isinstance(start, int):
            start = pl.multiple_of(start, 16)
        return own[which].at[pl.ds(start, size), columns]

    def hop(which, kind, order, stage, mask):
        bit = orders[order][stage]
        shard = flip(me, mask)
        source = own_part(which, kind, order) if mask == 0 else part(which, shard, kind, order)
        send(
            (which, kind, order, stage, mask), source, part(which, shard, kind, order),
            part(which, flip(shard, bit), kind, order), (flip(me, bit), row),
        )

    def send_own(which, kind):
        for stage in range(bits - 1):
            for order in range(2):
                hop(which, kind, order, stage, 0)

    def share(which, kind, mask):
        shard = flip(me, mask)
        source = part(which, shard, kind) if mask else own[which]
        send(
            (which, kind, "s", mask), source, part(which, shard, kind),
            part(which, flip(shard, 1), kind), sibling,
        )

    even_masks = range(2, n_clip, 2)

    def pump(which, kind, depth):
        for order in range(2):
            line = orders[order]
            for stage in range(bits - 1):
                earlier = sum(line[:stage])
                for mask in range(0, n_clip, 2):
                    gained = mask | line[stage]
                    if mask & ~earlier or gained.bit_count() != depth:
                        continue
                    arrivals[which, kind, order, stage, mask].wait_recv()
                    for later in range(stage + 1, bits - 1):
                        hop(which, kind, order, later, gained)
        for mask in even_masks:
            if mask.bit_count() == depth:
                if kind == "mine":
                    shard = flip(me, mask)
                    send(
                        (which, "z", mask), part(which, shard, "mine"),
                        part(which, shard, "mine"), part(which, shard, "theirs"), layer,
                    )
                share(which, kind, mask)

    def settle(which, depth):
        for mask in even_masks:
            if mask.bit_count() == depth:
                arrivals[which, "z", mask].wait_recv()
                share(which, "theirs", mask)

    def from_sibling(which, masks):
        for mask in masks:
            for kind in ("mine", "direct", "theirs") if mask else ("all",):
                arrivals[which, kind, "s", mask].wait_recv()

    def edge_copy(slot, source_row, target, device):
        return pltpu.make_async_remote_copy(
            src_ref=clips.at[0, pl.ds(0, used), source_row], dst_ref=halo.at[target],
            send_sem=local_sems.at[2 + slot], recv_sem=local_sems.at[4 + slot],
            device_id=device, device_id_type=MESH,
        )

    down = edge_copy(0, height - 1, 0, (me, lax.rem(row + 1, n_row)))
    up = edge_copy(1, 0, 1, (me, lax.rem(row + n_row - 1, n_row)))
    has_above, has_below = row > 0, row < n_row - 1

    send_own(0, "mine")
    pl.when(has_below)(down.start)
    pl.when(has_above)(up.start)
    send_own(0, "direct")
    share(0, "all", 0)
    locals_ = [
        pltpu.make_async_copy(own[w], part(w, me, "all"), local_sems.at[w]) for w in range(2)
    ]
    for copy in locals_:
        copy.start()

    fetch.wait()
    for copy in vectors:
        copy.wait()

    tiles = frames * height
    population = tiles * cols * group_width

    def tile(index):
        return x[0, index // height, index % height].astype(jnp.float32)

    def fold(values):
        return jnp.sum(values.reshape(cols // 8, 8, channels), axis=0)

    zeros = jnp.zeros((8, channels), jnp.float32)
    total = lax.fori_loop(0, tiles, lambda k, s: s + fold(tile(k)), zeros, unroll=2)
    total = jnp.broadcast_to(jnp.sum(total, axis=0, keepdims=True), (8, channels))
    near_mean = group_total(total, group_width) / population

    def squares(k, s):
        centred = tile(k) - near_mean[:1]
        return s + fold(centred * centred)

    square = lax.fori_loop(0, tiles, squares, zeros, unroll=2)
    square = jnp.broadcast_to(jnp.sum(square, axis=0, keepdims=True), (8, channels))
    near_square = group_total(square, group_width)
    line = lax.broadcasted_iota(jnp.int32, (8, channels), 0)
    stats[0] = jnp.where(line < 4, near_mean, near_square)
    for d in range(1, n_row):
        send(("stats", d), stats.at[0], stats.at[d], stats.at[d], (me, lax.rem(row + d, n_row)))

    pump(0, "mine", 1)
    send_own(1, "mine")

    for d in range(1, n_row):
        arrivals["stats", d].wait_recv()
    means = [stats[d, 0:1] for d in range(n_row)]
    mean = sum(means) / n_row
    spread = sum(stats[d, 4:5] for d in range(n_row))
    spread = spread + population * sum((m - mean) * (m - mean) for m in means)
    inverse = lax.rsqrt(spread / (population * n_row) + 1e-06)

    place = lax.broadcasted_iota(jnp.int32, (cols, channels), 0)

    def put(frame, line, values):
        for b, moved in enumerate((
            jnp.where(place == 0, 0.0, pltpu.roll(values, 1, 0)),
            values,
            jnp.where(place == cols - 1, 0.0, pltpu.roll(values, cols - 1, 0)),
        )):
            moved = moved.astype(jnp.bfloat16)
            for c in range(2):
                act[b, c, frame, line] = moved[:, c * half:(c + 1) * half]

    def activate(values):
        normed = (values - mean) * inverse * gain[...] + bias[...]
        return normed / (1.0 + jnp.exp(-normed))

    @pl.loop(0, used * height)
    def _(index):
        frame, line = index // height, index % height
        put(frame, line + 1, activate(x[0, frame, line].astype(jnp.float32)))

    pump(0, "direct", 1)
    send_own(1, "direct")
    share(1, "all", 0)
    for depth in range(2, bits):
        pump(0, "mine", depth)

    for present, copy, target in ((has_above, down, 0), (has_below, up, 1)):
        line = target * (height + 1)

        @pl.when(present)
        def _():
            copy.wait_recv()

            @pl.loop(0, used)
            def _(frame):
                put(frame, line, activate(halo[target, frame].astype(jnp.float32)))

        @pl.when(jnp.logical_not(present))
        def _():
            @pl.loop(0, used)
            def _(frame):
                for b in range(3):
                    for c in range(2):
                        act[b, c, frame, line] = jnp.zeros((cols, half), jnp.bfloat16)

    quarter = me // (n_clip // 4)

    def convolve(phase, blocks):
        @pl.loop(0, used)
        def _(frame):
            value = None
            for block in blocks:
                tap, c = block // 2, block % 2
                window = act[tap % 3, c, frame, pl.ds(tap // 3, height)]
                rows = pl.ds(pl.multiple_of(block * half, half), half)
                product = jnp.dot(
                    window.reshape(height * cols, half), spatial_full[rows, :],
                    preferred_element_type=jnp.float32,
                )
                value = product if value is None else value + product
            acc[frame] = value + (spatial_bias[...] if phase == 0 else acc[frame])

    def blocks_of(phase):
        spot = quarter
        if phase & 1:
            spot = spot + 1 - 2 * (spot % 2)
        if phase & 2:
            spot = (spot + 2) % 4
        first = (9 * spot + 1) // 2
        chosen = [first + k for k in range(4)]
        if phase & 1:
            chosen.append(spot // 2 * 9 + 4)
        return chosen

    def of_phase(phase):
        return [m for m in range(0, n_clip, 2) if m >> (bits - 2) == phase]

    locals_[0].wait()
    early = n_clip == 8
    if early:
        from_sibling(0, of_phase(0))
        convolve(0, blocks_of(0))
    pump(1, "mine", 1)
    for depth in range(2, bits):
        pump(0, "direct", depth)
    for depth in range(1, bits):
        settle(0, depth)
    pump(1, "direct", 1)
    for depth in range(2, bits):
        pump(1, "mine", depth)
    if not early:
        from_sibling(0, of_phase(0))
        convolve(0, blocks_of(0))
    for phase in (1, 2):
        from_sibling(0, of_phase(phase))
        convolve(phase, blocks_of(phase))
    for depth in range(2, bits):
        pump(1, "direct", depth)
    for depth in range(1, bits):
        settle(1, depth)
    from_sibling(0, of_phase(3))
    convolve(3, blocks_of(3))

    locals_[1].wait()
    from_sibling(1, range(0, n_clip, 2))

    def tap_product(k, frame):
        return jnp.dot(
            acc[frame].astype(jnp.bfloat16), temporal_full[k * channels:(k + 1) * channels, :],
            preferred_element_type=jnp.float32,
        )

    for j in range(frames // 2):
        before, at = max(2 * j - 1, 0), 2 * j
        pooled = 0.5 * (x[0, before].astype(jnp.float32) + x[0, at].astype(jnp.float32))
        value = sum(tap_product(k, max(2 * j + k - 2, 0)) for k in range(3))
        value = value + temporal_bias[...] + pooled.reshape(height * cols, channels)
        out[0, j] = value.reshape(height, cols, channels).astype(out.dtype)

    for copy in departures:
        copy.wait_send()
    pl.when(has_below)(down.wait_send)
    pl.when(has_above)(up.wait_send)


def body(
    n_clip, n_row,
    video_clips, norm_gain, norm_bias, spatial_weight, spatial_bias, temporal_weight, temporal_bias,
):
    _, frames, height, cols, channels = video_clips.shape
    used = frames - 1
    half = channels // 2
    shards = n_clip // 2 - 1
    copies = 2 * (4 * shards + shards + 3 * shards + 1) + n_row - 1
    vmem = pl.BlockSpec(memory_space=pltpu.VMEM)
    hbm = pl.BlockSpec(memory_space=pl.ANY)
    flat = lambda v: v.reshape(1, channels)
    return pl.pallas_call(
        functools.partial(kernel, n_clip, n_row),
        out_shape=jax.ShapeDtypeStruct((1, frames // 2, height, cols, channels), jnp.bfloat16),
        in_specs=[hbm] * 7,
        out_specs=vmem,
        scratch_shapes=[
            pltpu.VMEM((1, frames, height, cols, channels), jnp.bfloat16),
            pltpu.VMEM((1, channels), jnp.float32),
            pltpu.VMEM((1, channels), jnp.float32),
            pltpu.VMEM((1, channels), jnp.float32),
            pltpu.VMEM((1, channels), jnp.float32),
            pltpu.VMEM((9 * channels, channels), jnp.bfloat16),
            pltpu.VMEM((3 * channels, channels), jnp.bfloat16),
            pltpu.VMEM((3, 2, used, height + 2, cols, half), jnp.bfloat16),
            pltpu.VMEM((used, height * cols, channels), jnp.float32),
            pltpu.VMEM((2, used, cols, channels), jnp.bfloat16),
            pltpu.VMEM((n_row, 8, channels), jnp.float32),
            pltpu.SemaphoreType.DMA((copies,)),
            pltpu.SemaphoreType.DMA((copies,)),
            pltpu.SemaphoreType.DMA((11,)),
        ],
        compiler_params=pltpu.CompilerParams(
            collective_id=0, has_side_effects=True, vmem_limit_bytes=60 * 1024 * 1024
        ),
    )(
        video_clips, flat(norm_gain), flat(norm_bias), spatial_weight, flat(spatial_bias),
        temporal_weight, flat(temporal_bias),
    )


def solution(mesh):
    placed = (
        P("clip", None, "row", None, None),
        P(),
        P(),
        P("clip", None),
        P(),
        P("clip", None),
        P(),
    )
    return jax.shard_map(
        functools.partial(body, mesh.shape["clip"], mesh.shape["row"]),
        mesh=mesh,
        in_specs=placed,
        out_specs=P("clip", None, "row", None, None),
        check_vma=False,
    )
```

```python
import functools

import jax
import jax.numpy as jnp
from jax import lax
from jax.experimental import pallas as pl
from jax.experimental.pallas import tpu as pltpu
from jax.sharding import PartitionSpec as P

GROUPS = 32
MESH = pl.DeviceIdType.MESH


def group_total(values, group_width):
    lanes = values.shape[1]
    step = 1
    while step < group_width:
        values = values + pltpu.roll(values, step, 1)
        step *= 2
    lane = lax.broadcasted_iota(jnp.int32, values.shape, 1)
    values = jnp.where(lane % group_width == group_width - 1, values, 0.0)
    step = 1
    while step < group_width:
        values = values + pltpu.roll(values, lanes - step, 1)
        step *= 2
    return values


def z_rows(rows):
    return max(rows // 64 * 16, 16)


def kernel(
    n_clip, n_row,
    clips, gain_in, bias_in, spatial, spatial_bias_in, temporal, temporal_bias_in,
    out,
    x, gain, bias, spatial_bias, temporal_bias,
    spatial_full, temporal_full, act, acc, halo, stats,
    send_sems, recv_sems, local_sems, stat_sends, stat_recvs,
):
    me, row = lax.axis_index("clip"), lax.axis_index("row")
    parity = row % 2
    _, frames, height, cols, channels = clips.shape
    used = acc.shape[0]
    group_width = channels // GROUPS
    half = channels // 2
    bits = n_clip.bit_length() - 1
    chip_bits = [1 << k for k in range(1, bits)]
    orders = (chip_bits, chip_bits[::-1])
    own = (spatial, temporal)
    full = (spatial_full, temporal_full)

    def flip(index, mask):
        for k in range(bits):
            if mask >> k & 1:
                index = index + (1 - 2 * (index // (1 << k) % 2)) * (1 << k)
        return index

    sibling, layer = (flip(me, 1), row), (me, flip(row, 1))

    fetch = pltpu.make_async_copy(clips, x, local_sems.at[6])
    fetch.start()
    vectors = [
        pltpu.make_async_copy(source, target, local_sems.at[7 + k])
        for k, (source, target) in enumerate((
            (gain_in, gain), (bias_in, bias),
            (spatial_bias_in, spatial_bias), (temporal_bias_in, temporal_bias),
        ))
    ]
    for copy in vectors:
        copy.start()

    barrier = pltpu.get_barrier_semaphore()
    greeted = [(flip(me, 1 << k), row) for k in range(bits)]
    has_above, has_below = row > 0, row < n_row - 1
    above, below = (me, lax.rem(row + n_row - 1, n_row)), (me, lax.rem(row + 1, n_row))

    def greet(device):
        pl.semaphore_signal(barrier, inc=1, device_id=device, device_id_type=MESH)

    for device in greeted:
        greet(device)
    pl.when(has_above)(lambda: greet(above))
    pl.when(has_below)(lambda: greet(below))
    pl.semaphore_wait(
        barrier, len(greeted) + has_above.astype(jnp.int32) + has_below.astype(jnp.int32)
    )

    arrivals, departures = {}, []

    def send(key, source, target, landing, device):
        slot = len(departures)
        copy = pltpu.make_async_remote_copy(
            src_ref=source, dst_ref=target, send_sem=send_sems.at[slot],
            recv_sem=recv_sems.at[slot], device_id=device, device_id_type=MESH,
        )
        copy.start()
        departures.append(copy)
        arrivals[key] = pltpu.make_async_remote_copy(
            src_ref=landing, dst_ref=landing, send_sem=send_sems.at[slot],
            recv_sem=recv_sems.at[slot], device_id=device, device_id_type=MESH,
        )

    def span(which, kind):
        rows = own[which].shape[0]
        edge = z_rows(rows)
        if kind == "mine":
            return parity * (rows - edge), edge
        if kind == "theirs":
            return (1 - parity) * (rows - edge), edge
        if kind == "direct":
            return edge, rows - 2 * edge
        return 0, rows

    def part(which, shard, kind, order=None):
        start, size = span(which, kind)
        base = pl.multiple_of(shard * own[which].shape[0] + start, 16)
        columns = slice(None) if order is None else pl.ds(order * half, half)
        return full[which].at[pl.ds(base, size), columns]

    def own_part(which, kind, order=None):
        start, size = span(which, kind)
        columns = slice(None) if order is None else pl.ds(order * half, half)
        if not isinstance(start, int):
            start = pl.multiple_of(start, 16)
        return own[which].at[pl.ds(start, size), columns]

    def hop(which, kind, order, stage, mask):
        bit = orders[order][stage]
        shard = flip(me, mask)
        source = own_part(which, kind, order) if mask == 0 else part(which, shard, kind, order)
        send(
            (which, kind, order, stage, mask), source, part(which, shard, kind, order),
            part(which, flip(shard, bit), kind, order), (flip(me, bit), row),
        )

    def send_own(which, kind):
        for stage in range(bits - 1):
            for order in range(2):
                hop(which, kind, order, stage, 0)

    def share(which, kind, mask):
        shard = flip(me, mask)
        source = part(which, shard, kind) if mask else own[which]
        send(
            (which, kind, "s", mask), source, part(which, shard, kind),
            part(which, flip(shard, 1), kind), sibling,
        )

    even_masks = range(2, n_clip, 2)

    def pump(which, kind, depth):
        for order in range(2):
            line = orders[order]
            for stage in range(bits - 1):
                earlier = sum(line[:stage])
                for mask in range(0, n_clip, 2):
                    gained = mask | line[stage]
                    if mask & ~earlier or gained.bit_count() != depth:
                        continue
                    arrivals[which, kind, order, stage, mask].wait_recv()
                    for later in range(stage + 1, bits - 1):
                        hop(which, kind, order, later, gained)
        for mask in even_masks:
            if mask.bit_count() == depth:
                if kind == "mine":
                    shard = flip(me, mask)
                    send(
                        (which, "z", mask), part(which, shard, "mine"),
                        part(which, shard, "mine"), part(which, shard, "theirs"), layer,
                    )
                share(which, kind, mask)

    def settle(which, depth):
        for mask in even_masks:
            if mask.bit_count() == depth:
                arrivals[which, "z", mask].wait_recv()
                share(which, "theirs", mask)

    def from_sibling(which, masks):
        for mask in masks:
            for kind in ("mine", "direct", "theirs") if mask else ("all",):
                arrivals[which, kind, "s", mask].wait_recv()

    def edge_copy(slot, source_row, target, device):
        return pltpu.make_async_remote_copy(
            src_ref=clips.at[0, pl.ds(0, used), source_row], dst_ref=halo.at[target],
            send_sem=local_sems.at[2 + slot], recv_sem=local_sems.at[4 + slot],
            device_id=device, device_id_type=MESH,
        )

    down = edge_copy(0, height - 1, 0, below)
    up = edge_copy(1, 0, 1, above)

    send_own(0, "mine")
    pl.when(has_below)(down.start)
    pl.when(has_above)(up.start)
    send_own(0, "direct")
    share(0, "all", 0)
    locals_ = [
        pltpu.make_async_copy(own[w], part(w, me, "all"), local_sems.at[w]) for w in range(2)
    ]
    for copy in locals_:
        copy.start()

    fetch.wait()
    for copy in vectors:
        copy.wait()

    tiles = frames * height
    population = tiles * cols * group_width

    def tile(index):
        return x[0, index // height, index % height].astype(jnp.float32)

    def fold(values):
        return jnp.sum(values.reshape(cols // 8, 8, channels), axis=0)

    zeros = jnp.zeros((8, channels), jnp.float32)
    total = lax.fori_loop(0, tiles, lambda k, s: s + fold(tile(k)), zeros, unroll=2)
    total = jnp.broadcast_to(jnp.sum(total, axis=0, keepdims=True), (8, channels))
    near_mean = group_total(total, group_width) / population

    def squares(k, s):
        centred = tile(k) - near_mean[:1]
        return s + fold(centred * centred)

    square = lax.fori_loop(0, tiles, squares, zeros, unroll=2)
    square = jnp.broadcast_to(jnp.sum(square, axis=0, keepdims=True), (8, channels))
    near_square = group_total(square, group_width)
    line = lax.broadcasted_iota(jnp.int32, (8, channels), 0)
    stats[row] = jnp.where(line < 4, near_mean, near_square)

    def passing(way, k, source):
        slot = way * (n_row - 1) + k
        where = stats.at[lax.rem(source + n_row, n_row)]
        return pltpu.make_async_remote_copy(
            src_ref=where, dst_ref=where, send_sem=stat_sends.at[slot],
            recv_sem=stat_recvs.at[slot], device_id=(below, above)[way], device_id_type=MESH,
        )

    goes, comes = [], []
    for k in range(n_row - 1):
        goes.append((
            (jnp.logical_and(row >= k, has_below), passing(0, k, row - k)),
            (jnp.logical_and(row + k < n_row, has_above), passing(1, k, row + k)),
        ))
        comes.append((
            (row - 1 - k >= 0, passing(0, k, row - 1 - k)),
            (row + 1 + k < n_row, passing(1, k, row + 1 + k)),
        ))
    for present, copy in goes[0]:
        pl.when(present)(copy.start)

    pump(0, "mine", 1)
    send_own(1, "mine")

    for k in range(n_row - 1):
        for present, copy in comes[k]:
            pl.when(present)(copy.wait_recv)
        if k + 1 < n_row - 1:
            for present, copy in goes[k + 1]:
                pl.when(present)(copy.start)
    means = [stats[d, 0:1] for d in range(n_row)]
    mean = sum(means) / n_row
    spread = sum(stats[d, 4:5] for d in range(n_row))
    spread = spread + population * sum((m - mean) * (m - mean) for m in means)
    inverse = lax.rsqrt(spread / (population * n_row) + 1e-06)

    place = lax.broadcasted_iota(jnp.int32, (cols, channels), 0)

    def put(frame, line, values):
        for b, moved in enumerate((
            jnp.where(place == 0, 0.0, pltpu.roll(values, 1, 0)),
            values,
            jnp.where(place == cols - 1, 0.0, pltpu.roll(values, cols - 1, 0)),
        )):
            moved = moved.astype(jnp.bfloat16)
            for c in range(2):
                act[b, c, frame, line] = moved[:, c * half:(c + 1) * half]

    def activate(values):
        normed = (values - mean) * inverse * gain[...] + bias[...]
        return normed / (1.0 + jnp.exp(-normed))

    @pl.loop(0, used * height)
    def _(index):
        frame, line = index // height, index % height
        put(frame, line + 1, activate(x[0, frame, line].astype(jnp.float32)))

    pump(0, "direct", 1)
    send_own(1, "direct")
    share(1, "all", 0)
    for depth in range(2, bits):
        pump(0, "mine", depth)

    for present, copy, target in ((has_above, down, 0), (has_below, up, 1)):
        line = target * (height + 1)

        @pl.when(present)
        def _():
            copy.wait_recv()

            @pl.loop(0, used)
            def _(frame):
                put(frame, line, activate(halo[target, frame].astype(jnp.float32)))

        @pl.when(jnp.logical_not(present))
        def _():
            @pl.loop(0, used)
            def _(frame):
                for b in range(3):
                    for c in range(2):
                        act[b, c, frame, line] = jnp.zeros((cols, half), jnp.bfloat16)

    quarter = me // (n_clip // 4)

    def convolve(phase, blocks):
        @pl.loop(0, used)
        def _(frame):
            value = None
            for block in blocks:
                tap, c = block // 2, block % 2
                window = act[tap % 3, c, frame, pl.ds(tap // 3, height)]
                rows = pl.ds(pl.multiple_of(block * half, half), half)
                product = jnp.dot(
                    window.reshape(height * cols, half), spatial_full[rows, :],
                    preferred_element_type=jnp.float32,
                )
                value = product if value is None else value + product
            acc[frame] = value + (spatial_bias[...] if phase == 0 else acc[frame])

    def blocks_of(phase):
        spot = quarter
        if phase & 1:
            spot = spot + 1 - 2 * (spot % 2)
        if phase & 2:
            spot = (spot + 2) % 4
        first = (9 * spot + 1) // 2
        chosen = [first + k for k in range(4)]
        if phase & 1:
            chosen.append(spot // 2 * 9 + 4)
        return chosen

    def of_phase(phase):
        return [m for m in range(0, n_clip, 2) if m >> (bits - 2) == phase]

    locals_[0].wait()
    early = n_clip == 8
    if early:
        from_sibling(0, of_phase(0))
        convolve(0, blocks_of(0))
    pump(1, "mine", 1)
    for depth in range(2, bits):
        pump(0, "direct", depth)
    for depth in range(1, bits):
        settle(0, depth)
    pump(1, "direct", 1)
    for depth in range(2, bits):
        pump(1, "mine", depth)
    if not early:
        from_sibling(0, of_phase(0))
        convolve(0, blocks_of(0))
    for phase in (1, 2):
        from_sibling(0, of_phase(phase))
        convolve(phase, blocks_of(phase))
    for depth in range(2, bits):
        pump(1, "direct", depth)
    for depth in range(1, bits):
        settle(1, depth)
    from_sibling(0, of_phase(3))
    convolve(3, blocks_of(3))

    locals_[1].wait()
    from_sibling(1, range(0, n_clip, 2))

    def tap_product(k, frame):
        return jnp.dot(
            acc[frame].astype(jnp.bfloat16), temporal_full[k * channels:(k + 1) * channels, :],
            preferred_element_type=jnp.float32,
        )

    for j in range(frames // 2):
        before, at = max(2 * j - 1, 0), 2 * j
        pooled = 0.5 * (x[0, before].astype(jnp.float32) + x[0, at].astype(jnp.float32))
        value = sum(tap_product(k, max(2 * j + k - 2, 0)) for k in range(3))
        value = value + temporal_bias[...] + pooled.reshape(height * cols, channels)
        out[0, j] = value.reshape(height, cols, channels).astype(out.dtype)

    for copy in departures:
        copy.wait_send()
    for pair in goes:
        for present, copy in pair:
            pl.when(present)(copy.wait_send)
    pl.when(has_below)(down.wait_send)
    pl.when(has_above)(up.wait_send)


def body(
    n_clip, n_row,
    video_clips, norm_gain, norm_bias, spatial_weight, spatial_bias, temporal_weight, temporal_bias,
):
    _, frames, height, cols, channels = video_clips.shape
    used = frames - 1
    half = channels // 2
    shards = n_clip // 2 - 1
    copies = 2 * (4 * shards + shards + 3 * shards + 1)
    vmem = pl.BlockSpec(memory_space=pltpu.VMEM)
    hbm = pl.BlockSpec(memory_space=pl.ANY)
    flat = lambda v: v.reshape(1, channels)
    return pl.pallas_call(
        functools.partial(kernel, n_clip, n_row),
        out_shape=jax.ShapeDtypeStruct((1, frames // 2, height, cols, channels), jnp.bfloat16),
        in_specs=[hbm] * 7,
        out_specs=vmem,
        scratch_shapes=[
            pltpu.VMEM((1, frames, height, cols, channels), jnp.bfloat16),
            pltpu.VMEM((1, channels), jnp.float32),
            pltpu.VMEM((1, channels), jnp.float32),
            pltpu.VMEM((1, channels), jnp.float32),
            pltpu.VMEM((1, channels), jnp.float32),
            pltpu.VMEM((9 * channels, channels), jnp.bfloat16),
            pltpu.VMEM((3 * channels, channels), jnp.bfloat16),
            pltpu.VMEM((3, 2, used, height + 2, cols, half), jnp.bfloat16),
            pltpu.VMEM((used, height * cols, channels), jnp.float32),
            pltpu.VMEM((2, used, cols, channels), jnp.bfloat16),
            pltpu.VMEM((n_row, 8, channels), jnp.float32),
            pltpu.SemaphoreType.DMA((copies,)),
            pltpu.SemaphoreType.DMA((copies,)),
            pltpu.SemaphoreType.DMA((11,)),
            pltpu.SemaphoreType.DMA((2 * (n_row - 1),)),
            pltpu.SemaphoreType.DMA((2 * (n_row - 1),)),
        ],
        compiler_params=pltpu.CompilerParams(
            collective_id=0, has_side_effects=True, vmem_limit_bytes=60 * 1024 * 1024
        ),
    )(
        video_clips, flat(norm_gain), flat(norm_bias), spatial_weight, flat(spatial_bias),
        temporal_weight, flat(temporal_bias),
    )


def solution(mesh):
    placed = (
        P("clip", None, "row", None, None),
        P(),
        P(),
        P("clip", None),
        P(),
        P("clip", None),
        P(),
    )
    return jax.shard_map(
        functools.partial(body, mesh.shape["clip"], mesh.shape["row"]),
        mesh=mesh,
        in_specs=placed,
        out_specs=P("clip", None, "row", None, None),
        check_vma=False,
    )
```
